32 devices in a mesh: groups: 2 (over y), dp: 4 (over z), mp: 2 (over x), pair: 2 (over core).
Axes of the slice: x: 2, y: 2, z: 4, core: 2. Of those that a mesh axis runs over, the one named last changes fastest.
Arguments:
- image_features: bfloat16 [2048, 1152], P(('groups', 'dp')), parts along dimension 0, may hold values from -6 to 6
- text_features: bfloat16 [2048, 1152], P(('groups', 'dp')), parts along dimension 0, may hold values from -6 to 6
- image_head: bfloat16 [1152, 1152], P(None, ('mp', 'pair')), may hold values from -0.0048828125 to 0.0048828125
- text_head: bfloat16 [1152, 1152], P(None, ('mp', 'pair')), may hold values from -0.0048828125 to 0.0048828125
- log_scale: float32 [1], replicated, may hold values from 1.6 to 2.6
- bias: float32 [1], replicated, may hold values from -3 to -1
Outputs:
- row_loss: float32 [2048], P(('groups', 'dp')), parts along dimension 0
- image_head_grad: float32 [2304, 1152], P(('groups', 'dp'), ('mp', 'pair')), parts along dimension 0
- text_head_grad: float32 [2304, 1152], P(('groups', 'dp'), ('mp', 'pair')), parts along dimension 0
The draws below stay inside these ranges and needn't reach their ends.
There are 2 independent parts, one for each index of `groups`. The reference program is written for one: setup_inputs(seed, part) draws one part's arguments, and reference() takes and returns one part's arrays. A program takes and returns all parts, laid end to end along the dimension named above; an argument that names none is the same for every part. Nothing has to cross between parts.
All inputs are finite; a program needn't handle non-finite values.
Results may differ from the reference program's by a relative error of at most 0.0049.
Values may be sent and summed in bfloat16 or wider, within the bound.
A program may use at most 64 MiB of HBM per device.

```python
import jax
import jax.numpy as jnp
from jax import lax

D = 1152
E = 1152
ROWS = 256
BATCH = 1024
N_DP = 4


def spiked(drawn, key, source, target, shards_of, factor):
    def block_of(position):
        return (jnp.arange(drawn.shape[position]) // (drawn.shape[position] // shards_of)).reshape((-1,) + (1,) * (drawn.ndim - 1 - position))

    one_side = jax.random.permutation(key, shards_of)[block_of(target)]
    other_side = (block_of(target) + shards_of // 2) % shards_of
    return jnp.where((block_of(source) == one_side) | (block_of(source) == other_side), factor * drawn, drawn)


def level_of(stream_key, extent, shards, least, top_value):
    def one(position, shards_of):
        steps = jax.random.uniform(jax.random.fold_in(jax.random.fold_in(stream_key, 6), position), (shards_of,), jnp.float32, least / len(shards), top_value / len(shards))
        return jnp.repeat(jnp.exp(steps), extent[position] // shards_of).reshape((-1,) + (1,) * (len(extent) - position - 1))

    loudness = one(*shards[0])
    for cut in shards[1:]:
        loudness = loudness * one(*cut)
    return loudness


def centred(own_key, dims, deviation, reach, pieces=(), kind=jnp.bfloat16):
    level = level_of(own_key, dims, pieces, -0.22, 0.18) if pieces else 1.0
    result = jax.random.normal(own_key, dims, jnp.float32) * deviation * level
    return jnp.minimum(jnp.maximum(result, -reach), reach).astype(kind)


def bell_draw_with(rng, dims, deviation, most, shards, heavy, kind=jnp.bfloat16):
    drawn = deviation * jax.random.normal(rng, dims, jnp.float32)
    if shards:
        drawn = drawn * level_of(rng, dims, shards, -0.22, 0.18)
    return jnp.clip(spiked(drawn, jax.random.fold_in(rng, 3), *heavy), -most, most).astype(kind)


def setup_inputs(seed: int = 0, part: int = 0) -> dict:
    seeds = jax.random.split(jax.random.key(seed), 7)
    part_keys = jax.random.split(jax.random.fold_in(seeds[6], part), 7)
    image_features = bell_draw_with(part_keys[0], (BATCH, E), 1.0, 6.0, ((0, 4),), (0, 1, 4, 2.0))
    text_features = bell_draw_with(part_keys[1], (BATCH, E), 1.0, 6.0, ((0, 4),), (0, 1, 4, 2.0))
    image_head = centred(seeds[2], (E, D), (E * D) ** -0.5, 0.0048828125, ((1, 4),))
    text_head = centred(seeds[3], (E, D), (E * D) ** -0.5, 0.0048828125, ((1, 4),))
    log_scale = jnp.clip(jax.random.uniform(seeds[4], (1,), jnp.float32, 1.6, 2.6), 1.6, 2.6)
    bias = jnp.clip(jax.random.uniform(seeds[5], (1,), jnp.float32, -3.0, -1.0), -3.0, -1.0)
    return dict(image_features=image_features, text_features=text_features, image_head=image_head, text_head=text_head, log_scale=log_scale, bias=bias)


epsilon = 1e-06

def embed(features, head):
    projected = jnp.dot(features, head, preferred_element_type=jnp.float32)
    norm_rows = jnp.sqrt(lax.optimization_barrier(jnp.sum(projected * projected, axis=1, keepdims=True)) + epsilon)
    unit_rows = projected / norm_rows
    return (norm_rows, unit_rows, unit_rows.astype(jnp.bfloat16))

def backward(unit_rows, norm_rows, gradient):
    inner = lax.optimization_barrier(jnp.sum(unit_rows * gradient, axis=1, keepdims=True))
    return ((gradient - unit_rows * inner) / norm_rows).astype(jnp.bfloat16)

def reference(image_features, text_features, image_head, text_head, log_scale, bias):
    total = ROWS * N_DP
    norm_image, unit_image, emb_image = embed(image_features, image_head)
    norm_text, unit_text, emb_text = embed(text_features, text_head)
    scale = jnp.exp(log_scale[0])
    offset = bias[0]
    columns = lax.broadcasted_iota(jnp.int32, (ROWS, total), 1)
    local_rows = lax.broadcasted_iota(jnp.int32, (ROWS, total), 0)

    def block_step(grad_text, inputs):
        emb_block, start = inputs
        similarity = jnp.dot(emb_block, emb_text.T, preferred_element_type=jnp.float32)
        logits = scale * similarity + offset
        signs = jnp.where(local_rows + start == columns, jnp.float32(1.0), jnp.float32(-1.0))
        loss = lax.optimization_barrier(jnp.sum(jax.nn.softplus(-signs * logits), axis=1)) / total
        weights = (-signs * jax.nn.sigmoid(-signs * logits) * (scale / ROWS)).astype(jnp.bfloat16)
        grad_block = jnp.dot(weights, emb_text, preferred_element_type=jnp.float32)
        grad_text = grad_text + jnp.dot(weights.T, emb_block, preferred_element_type=jnp.float32)
        return (grad_text, (loss, grad_block))
    starts = (jnp.arange(N_DP) * ROWS).astype(jnp.int32)
    width = emb_image.shape[1]
    blocks = emb_image.reshape(N_DP, ROWS, width)
    grad_text, outputs = lax.scan(block_step, jnp.zeros((total, width), jnp.float32), (blocks, starts))
    row_loss = outputs[0].reshape(total)
    grad_image = outputs[1].reshape(total, width)
    back_image = backward(unit_image, norm_image, grad_image)
    back_text = backward(unit_text, norm_text, grad_text)
    image_head_grad = jnp.dot(image_features.T, back_image, preferred_element_type=jnp.float32)
    text_head_grad = jnp.dot(text_features.T, back_text, preferred_element_type=jnp.float32)
    return (row_loss, image_head_grad, text_head_grad)
```

```python
import functools

import jax
import jax.numpy as jnp
from jax import lax
from jax.experimental import pallas as pl
from jax.experimental.pallas import tpu as pltpu
from jax.sharding import PartitionSpec as P

epsilon = 1e-06
f32 = jnp.float32
bf16 = jnp.bfloat16
MESH = pl.DeviceIdType.MESH


def dot_nt(a, b):
    return lax.dot_general(a, b, (((1,), (1,)), ((), ())), preferred_element_type=f32)


def dot_tn(a, b):
    return lax.dot_general(a, b, (((0,), (0,)), ((), ())), preferred_element_type=f32)


def dot_nn(a, b):
    return jnp.dot(a, b, preferred_element_type=f32)


def as_rows(first, second):
    lanes = lax.broadcasted_iota(jnp.int32, (first.shape[0], 128), 1)
    wide = jnp.where(lanes == 0, first, jnp.where(lanes == 1, second, 0.0))
    return wide.T[:8]


def as_columns(block):
    wide = jnp.concatenate([block, jnp.zeros((120, block.shape[1]), f32)], axis=0).T
    return wide[:, 0:1], wide[:, 1:2]


def kernel(
    n, mp, pair,
    scalars, xi, xt, hi, ht, xti, xtt,
    loss_out, gi_out, gt_out,
    unit_i, unit_t, image, text, tall, wall, gi_send, gi_recv, gt_send, gt_recv, own_gt,
    ts_send, ts_recv, stat_send, stat_recv, head_send, head_recv,
    s_send, s_recv, d_send, d_recv,
):
    shards = mp * pair
    rows = xi.shape[0]
    part = rows // shards
    width = hi.shape[1]
    my_d = lax.axis_index("dp")
    my_s = lax.axis_index("mp") * pair + lax.axis_index("pair")
    offsets = [0] + [((k + 1) // 2) * (1 if k % 2 else -1) % n for k in range(1, n)]

    def ahead(k):
        return lax.rem(my_d + offsets[k], n)

    def behind(k):
        return lax.rem(my_d + n - offsets[k], n)

    def shard_up(k):
        return lax.rem(my_s + k, shards)

    def shard_down(k):
        return lax.rem(my_s + shards - k, shards)

    def shard_id(s):
        return {"mp": s // pair, "pair": lax.rem(s, pair)}

    def to_shard(src, dst, stage, k, s):
        copy = pltpu.make_async_remote_copy(
            src_ref=src, dst_ref=dst, send_sem=s_send.at[stage, k], recv_sem=s_recv.at[stage, k],
            device_id=shard_id(s), device_id_type=MESH)
        copy.start()
        return copy

    def to_dp(src, dst, stage, k, d):
        copy = pltpu.make_async_remote_copy(
            src_ref=src, dst_ref=dst, send_sem=d_send.at[stage, k], recv_sem=d_recv.at[stage, k],
            device_id={"dp": d}, device_id_type=MESH)
        copy.start()
        return copy

    sent = []
    others = range(1, shards)
    peers = range(1, n)

    barrier = pltpu.get_barrier_semaphore()
    for k in others:
        pl.semaphore_signal(barrier, inc=1, device_id=shard_id(shard_up(k)), device_id_type=MESH)
    for k in peers:
        pl.semaphore_signal(barrier, inc=1, device_id={"dp": ahead(k)}, device_id_type=MESH)

    def stats_start(stage, first, second):
        stat_send[stage] = as_rows(first, second)
        return [
            to_shard(stat_send.at[stage], stat_recv.at[stage, k], stage, k, shard_up(k))
            for k in others
        ]

    def stats_total(stage, copies):
        total = stat_send[stage]
        for k, copy in zip(others, copies):
            copy.wait_recv()
            total = total + stat_recv[stage, k]
        sent.extend(copies)
        return total

    proj_i = dot_nn(xi[...], hi[...])
    proj_t = dot_nn(xt[...], ht[...])
    sq_i = jnp.sum(proj_i * proj_i, axis=1, keepdims=True)
    sq_t = jnp.sum(proj_t * proj_t, axis=1, keepdims=True)
    pl.semaphore_wait(barrier, shards - 1 + n - 1)
    total_i, total_t = as_columns(stats_total(0, stats_start(0, sq_i, sq_t)))
    norm_i = jnp.sqrt(total_i + epsilon)
    norm_t = jnp.sqrt(total_t + epsilon)
    unit_text = proj_t / norm_t
    unit_t[...] = unit_text
    text[...] = unit_text.astype(bf16).reshape(shards, part, width)
    text_copies = [
        to_shard(text.at[shard_up(k)], tall.at[0, k], 3, k, shard_up(k)) for k in others
    ]
    tall[0, 0] = text[my_s]
    unit_image = proj_i / norm_i
    unit_i[...] = unit_image
    image[0] = unit_image.astype(bf16)
    image_copies = [to_shard(image.at[0], image.at[k], 4, k, shard_up(k)) for k in others]

    for copy in text_copies:
        copy.wait_recv()
    tall_copies = [to_dp(tall.at[0], tall.at[k], 0, k, ahead(k)) for k in peers]
    for copy in image_copies:
        copy.wait_recv()
    sent += text_copies + image_copies + tall_copies

    scale = scalars[0]
    offset = scalars[1]
    row_ids = lax.broadcasted_iota(jnp.int32, (rows, part), 0)
    col_ids = lax.broadcasted_iota(jnp.int32, (rows, part), 1) + my_s * part
    loss = jnp.zeros((rows, 1), f32)
    gt_copies = []
    for k in range(n):
        if k:
            tall_copies[k - 1].wait_recv()
        dots = dot_nt(image[0], tall[k, 0])
        for j in others:
            dots = dots + dot_nt(image[j], tall[k, j])
        logits = scale * dots + offset
        if k == 0:
            flip = jnp.where(row_ids == col_ids, f32(-1.0), f32(1.0))
        else:
            flip = f32(1.0)
        z = flip * logits
        small = jnp.exp(-jnp.abs(z))
        loss = loss + jnp.sum(jnp.maximum(z, 0.0) + jnp.log1p(small), axis=1, keepdims=True)
        sigmoid = jnp.where(z >= 0, f32(1.0), small) / (1.0 + small)
        weights = (flip * sigmoid * (scale / rows)).astype(bf16)
        wall[:, k * part:(k + 1) * part] = weights
        for j in range(shards):
            update = dot_tn(weights, image[j])
            if k == 0:
                own_gt[j] = update
            else:
                gt_send[k, j] = update.astype(bf16)
        if k:
            gt_copies.append(to_dp(gt_send.at[k], gt_recv.at[k], 1, k, behind(k)))
    sent += gt_copies

    gi_copies = []
    for j in list(others) + [0]:
        grad = dot_nn(wall[...], tall[:, j].reshape(n * part, width))
        if j:
            gi_send[j] = grad.astype(bf16)
            gi_copies.append(to_shard(gi_send.at[j], gi_recv.at[j], 5, j, shard_down(j)))
    sent += gi_copies
    for j, copy in zip(others, gi_copies):
        copy.wait_recv()
        grad = grad + gi_recv[j].astype(f32)
    stat_copies = stats_start(1, jnp.sum(unit_i[...] * grad, axis=1, keepdims=True), loss)
    total = stats_total(1, stat_copies)
    loss_out[...] = total[1:2] / (rows * n)
    inner, _ = as_columns(total)
    back_i = ((grad - unit_i[...] * inner) / norm_i).astype(bf16)

    def head_terms(which, x, back):
        copies = []
        for k in peers:
            head_send[which, k] = dot_nn(x[ahead(k)], back).astype(bf16)
            copies.append(to_dp(
                head_send.at[which, k], head_recv.at[which, k], 2 + which, k, ahead(k)))
        sent.extend(copies)
        return dot_nn(x[my_d], back), copies

    head_i, head_i_copies = head_terms(0, xti, back_i)

    for copy in gt_copies:
        copy.wait_recv()
    ts_copies = []
    for j in list(others) + [0]:
        share = own_gt[j]
        for k in peers:
            share = share + gt_recv[k, j].astype(f32)
        if j:
            ts_send[j] = share.astype(bf16)
            ts_copies.append(to_shard(ts_send.at[j], ts_recv.at[my_s], 6, j, shard_down(j)))
        else:
            ts_recv[my_s] = share.astype(bf16)
    sent += ts_copies
    for copy in ts_copies:
        copy.wait_send()
    for j in others:
        pltpu.make_async_remote_copy(
            src_ref=ts_send.at[j], dst_ref=ts_recv.at[shard_up(j)], send_sem=s_send.at[6, j],
            recv_sem=s_recv.at[6, j], device_id=shard_id(shard_down(j)), device_id_type=MESH,
        ).wait_recv()
    grad_t = ts_recv[...].reshape(rows, width).astype(f32)
    inner_t = jnp.sum(unit_t[...] * grad_t, axis=1, keepdims=True)
    inner_t, _ = as_columns(stats_total(2, stats_start(2, inner_t, inner_t)))
    back_t = ((grad_t - unit_t[...] * inner_t) / norm_t).astype(bf16)
    head_t, head_t_copies = head_terms(1, xtt, back_t)

    high = gi_out.shape[0]
    for which, value, copies, out in (
        (0, head_i, head_i_copies, gi_out), (1, head_t, head_t_copies, gt_out)
    ):
        for k, copy in zip(peers, copies):
            copy.wait_recv()
            value = value + head_recv[which, k].astype(f32)
        out[...] = value[:high]
    for copy in sent:
        if not any(copy is done for done in ts_copies):
            copy.wait_send()


def body(image_features, text_features, image_head, text_head, log_scale, bias):
    rows, depth = image_features.shape
    width = image_head.shape[1]
    n, mp, pair = lax.axis_size("dp"), lax.axis_size("mp"), lax.axis_size("pair")
    shards = mp * pair
    part = rows // shards
    high = depth // n
    padded = -(-high // 16) * 16

    def turned(features):
        blocks = features.T.reshape(n, high, rows)
        return jnp.pad(blocks, ((0, 0), (0, padded - high), (0, 0)))

    scalars = jnp.concatenate([jnp.exp(log_scale), bias])
    vmem = pl.BlockSpec(memory_space=pltpu.VMEM)
    row_loss, gi, gt = pl.pallas_call(
        functools.partial(kernel, n, mp, pair),
        out_shape=(
            jax.ShapeDtypeStruct((1, rows), f32),
            jax.ShapeDtypeStruct((high, width), f32),
            jax.ShapeDtypeStruct((high, width), f32),
        ),
        in_specs=[pl.BlockSpec(memory_space=pltpu.SMEM)] + [vmem] * 6,
        out_specs=(vmem, vmem, vmem),
        scratch_shapes=[
            pltpu.VMEM((rows, width), f32),
            pltpu.VMEM((rows, width), f32),
            pltpu.VMEM((shards, rows, width), bf16),
            pltpu.VMEM((shards, part, width), bf16),
            pltpu.VMEM((n, shards, part, width), bf16),
            pltpu.VMEM((rows, n * part), bf16),
            pltpu.VMEM((shards, rows, width), bf16),
            pltpu.VMEM((shards, rows, width), bf16),
            pltpu.VMEM((n, shards, part, width), bf16),
            pltpu.VMEM((n, shards, part, width), bf16),
            pltpu.VMEM((shards, part, width), f32),
            pltpu.VMEM((shards, part, width), bf16),
            pltpu.VMEM((shards, part, width), bf16),
            pltpu.VMEM((3, 8, rows), f32),
            pltpu.VMEM((3, shards, 8, rows), f32),
            pltpu.VMEM((2, n, padded, width), bf16),
            pltpu.VMEM((2, n, padded, width), bf16),
            pltpu.SemaphoreType.DMA((7, shards)),
            pltpu.SemaphoreType.DMA((7, shards)),
            pltpu.SemaphoreType.DMA((4, n)),
            pltpu.SemaphoreType.DMA((4, n)),
        ],
        compiler_params=pltpu.CompilerParams(
            collective_id=0, has_side_effects=True, vmem_limit_bytes=56 * 1024 * 1024
        ),
    )(
        scalars, image_features, text_features, image_head, text_head,
        turned(image_features), turned(text_features),
    )
    return row_loss.reshape(rows), gi, gt


def solution(mesh):
    in_specs = (
        P(("groups", "dp"), None),
        P(("groups", "dp"), None),
        P(None, ("mp", "pair")),
        P(None, ("mp", "pair")),
        P(),
        P(),
    )
    out_specs = (
        P(("groups", "dp")),
        P(("groups", "dp"), ("mp", "pair")),
        P(("groups", "dp"), ("mp", "pair")),
    )
    return jax.shard_map(body, mesh=mesh, in_specs=in_specs, out_specs=out_specs, check_vma=False)
```

```python
import functools

import jax
import jax.numpy as jnp
from jax import lax
from jax.experimental import pallas as pl
from jax.experimental.pallas import tpu as pltpu
from jax.sharding import PartitionSpec as P

epsilon = 1e-06
f32 = jnp.float32
bf16 = jnp.bfloat16
MESH = pl.DeviceIdType.MESH


def dot_nt(a, b):
    return lax.dot_general(a, b, (((1,), (1,)), ((), ())), preferred_element_type=f32)


def dot_tn(a, b):
    return lax.dot_general(a, b, (((0,), (0,)), ((), ())), preferred_element_type=f32)


def dot_nn(a, b):
    return jnp.dot(a, b, preferred_element_type=f32)


def as_rows(first, second):
    lanes = lax.broadcasted_iota(jnp.int32, (first.shape[0], 128), 1)
    wide = jnp.where(lanes == 0, first, jnp.where(lanes == 1, second, 0.0))
    return wide.T[:8]


def as_columns(block):
    wide = jnp.concatenate([block, jnp.zeros((120, block.shape[1]), f32)], axis=0).T
    return wide[:, 0:1], wide[:, 1:2]


def packing(width):
    main = width // 128 * 128
    rest = width - main

    def groups(padded, high):
        if not rest:
            return []
        step = tail_rows(padded, width)
        starts = range(0, high, step)
        return [
            (low, min(low + step, high), j * rest, (j + 1) * rest) for j, low in enumerate(starts)
        ]

    return main, groups


def tail_rows(padded, width):
    main = width // 128 * 128
    rest = width - main
    return -(-padded // (main // rest * 8)) * 8 if rest else 0


def kernel(
    n, mp, pair,
    scalars, xi, xt, hi, ht,
    loss_out, gi_out, gt_out,
    unit_i, unit_t, image, text, pieces, wide_image, turned, tall, wall, gi_send, gi_recv, gt_send, gt_recv, own_gt,
    ts_send, ts_recv, stat_send, stat_recv, head_send, head_recv,
    s_send, s_recv, d_send, d_recv,
):
    shards = mp * pair
    rows = xi.shape[0]
    part = rows // shards
    width = hi.shape[0]
    high = gi_out.shape[0]
    my_d = lax.axis_index("dp")
    my_s = lax.axis_index("mp") * pair + lax.axis_index("pair")
    offsets = [0] + [((k + 1) // 2) * (1 if k % 2 else -1) % n for k in range(1, n)]

    def ahead(k):
        return lax.rem(my_d + offsets[k], n)

    def behind(k):
        return lax.rem(my_d + n - offsets[k], n)

    def shard_up(k):
        return lax.rem(my_s + k, shards)

    def shard_down(k):
        return lax.rem(my_s + shards - k, shards)

    def shard_id(s):
        return {"mp": s // pair, "pair": lax.rem(s, pair)}

    def to_shard(src, dst, stage, k, s):
        copy = pltpu.make_async_remote_copy(
            src_ref=src, dst_ref=dst, send_sem=s_send.at[stage, k], recv_sem=s_recv.at[stage, k],
            device_id=shard_id(s), device_id_type=MESH)
        copy.start()
        return copy

    def to_dp(src, dst, stage, k, d):
        copy = pltpu.make_async_remote_copy(
            src_ref=src, dst_ref=dst, send_sem=d_send.at[stage, k], recv_sem=d_recv.at[stage, k],
            device_id={"dp": d}, device_id_type=MESH)
        copy.start()
        return copy

    sent = []
    others = range(1, shards)
    peers = range(1, n)

    barrier = pltpu.get_barrier_semaphore()
    for k in others:
        pl.semaphore_signal(barrier, inc=1, device_id=shard_id(shard_up(k)), device_id_type=MESH)
    for k in peers:
        pl.semaphore_signal(barrier, inc=1, device_id={"dp": ahead(k)}, device_id_type=MESH)

    def stats_start(stage, first, second):
        stat_send[stage] = as_rows(first, second)
        return [
            to_shard(stat_send.at[stage], stat_recv.at[stage, k], stage, k, shard_up(k))
            for k in others
        ]

    def stats_total(stage, copies):
        total = stat_send[stage]
        for k, copy in zip(others, copies):
            copy.wait_recv()
            total = total + stat_recv[stage, k]
        sent.extend(copies)
        return total

    proj_i = dot_nt(xi[...], hi[...])
    proj_t = dot_nt(xt[...], ht[...])
    sq_i = jnp.sum(proj_i * proj_i, axis=1, keepdims=True)
    sq_t = jnp.sum(proj_t * proj_t, axis=1, keepdims=True)
    pl.semaphore_wait(barrier, shards - 1 + n - 1)
    total_i, total_t = as_columns(stats_total(0, stats_start(0, sq_i, sq_t)))
    norm_i = jnp.sqrt(total_i + epsilon)
    norm_t = jnp.sqrt(total_t + epsilon)
    unit_text = proj_t / norm_t
    unit_t[...] = unit_text
    text[...] = unit_text.astype(bf16).reshape(shards, part, width)
    text_copies = [
        to_shard(text.at[shard_up(k)], pieces.at[k], 3, k, shard_up(k)) for k in others
    ]
    tall[0, :, :width] = text[my_s]
    unit_image = proj_i / norm_i
    unit_i[...] = unit_image
    image[0] = unit_image.astype(bf16)
    image_copies = [to_shard(image.at[0], image.at[k], 4, k, shard_up(k)) for k in others]

    for k, copy in zip(others, text_copies):
        copy.wait_recv()
        tall[0, :, k * width:(k + 1) * width] = pieces[k]
    tall_copies = [to_dp(tall.at[0], tall.at[k], 0, k, ahead(k)) for k in peers]
    wide_image[:, :width] = image[0]
    for which, x in enumerate((xi, xt)):
        across = x[...].T
        for e in range(n):
            turned[which, e, :high] = across[e * high:(e + 1) * high]
    for k, copy in zip(others, image_copies):
        copy.wait_recv()
        wide_image[:, k * width:(k + 1) * width] = image[k]
    sent += text_copies + image_copies + tall_copies

    scale = scalars[0]
    offset = scalars[1]
    row_ids = lax.broadcasted_iota(jnp.int32, (rows, part), 0)
    col_ids = lax.broadcasted_iota(jnp.int32, (rows, part), 1) + my_s * part
    loss = jnp.zeros((rows, 1), f32)
    gt_copies = []
    for k in range(n):
        if k:
            tall_copies[k - 1].wait_recv()
        dots = dot_nt(wide_image[...], tall[k])
        logits = scale * dots + offset
        if k == 0:
            flip = jnp.where(row_ids == col_ids, f32(-1.0), f32(1.0))
        else:
            flip = f32(1.0)
        z = flip * logits
        small = jnp.exp(-jnp.abs(z))
        loss = loss + jnp.sum(jnp.maximum(z, 0.0) + jnp.log1p(small), axis=1, keepdims=True)
        sigmoid = jnp.where(z >= 0, f32(1.0), small) / (1.0 + small)
        weights = (flip * sigmoid * (scale / rows)).astype(bf16)
        wall[:, k * part:(k + 1) * part] = weights
        update = dot_tn(weights, wide_image[...])
        if k == 0:
            own_gt[...] = update
        else:
            gt_send[k] = update.astype(bf16)
            gt_copies.append(to_dp(gt_send.at[k], gt_recv.at[k], 1, k, behind(k)))
    sent += gt_copies

    gi_copies = []
    grad_all = dot_nn(wall[...], tall[...].reshape(n * part, shards * width))
    for j in list(others) + [0]:
        grad = grad_all[:, j * width:(j + 1) * width]
        if j:
            gi_send[j] = grad.astype(bf16)
            gi_copies.append(to_shard(gi_send.at[j], gi_recv.at[j], 5, j, shard_down(j)))
    sent += gi_copies
    for j, copy in zip(others, gi_copies):
        copy.wait_recv()
        grad = grad + gi_recv[j].astype(f32)
    stat_copies = stats_start(1, jnp.sum(unit_i[...] * grad, axis=1, keepdims=True), loss)
    total = stats_total(1, stat_copies)
    loss_out[...] = total[1:2] / (rows * n)
    inner, _ = as_columns(total)
    back_i = ((grad - unit_i[...] * inner) / norm_i).astype(bf16)

    main, groups = packing(width)
    padded = turned.shape[2]

    def head_terms(which, back):
        copies = []
        for k in peers:
            term = dot_nn(turned[which, ahead(k)], back).astype(bf16)
            head_send[which, k, :padded] = term[:, :main]
            for low, top, left, right in groups(padded, padded):
                head_send[which, k, padded:padded + top - low, left:right] = term[low:top, main:]
            copies.append(to_dp(
                head_send.at[which, k], head_recv.at[which, k], 2 + which, k, ahead(k)))
        sent.extend(copies)
        return dot_nn(turned[which, my_d], back), copies

    head_i, head_i_copies = head_terms(0, back_i)

    for copy in gt_copies:
        copy.wait_recv()
    ts_copies = []
    share_all = own_gt[...]
    for k in peers:
        share_all = share_all + gt_recv[k].astype(f32)
    for j in list(others) + [0]:
        share = share_all[:, j * width:(j + 1) * width]
        if j:
            ts_send[j] = share.astype(bf16)
            ts_copies.append(to_shard(ts_send.at[j], ts_recv.at[my_s], 6, j, shard_down(j)))
        else:
            ts_recv[my_s] = share.astype(bf16)
    sent += ts_copies
    for copy in ts_copies:
        copy.wait_send()
    for j in others:
        pltpu.make_async_remote_copy(
            src_ref=ts_send.at[j], dst_ref=ts_recv.at[shard_up(j)], send_sem=s_send.at[6, j],
            recv_sem=s_recv.at[6, j], device_id=shard_id(shard_down(j)), device_id_type=MESH,
        ).wait_recv()
    grad_t = ts_recv[...].reshape(rows, width).astype(f32)
    inner_t = jnp.sum(unit_t[...] * grad_t, axis=1, keepdims=True)
    inner_t, _ = as_columns(stats_total(2, stats_start(2, inner_t, inner_t)))
    back_t = ((grad_t - unit_t[...] * inner_t) / norm_t).astype(bf16)
    head_t, head_t_copies = head_terms(1, back_t)

    for which, value, copies, out in (
        (0, head_i, head_i_copies, gi_out), (1, head_t, head_t_copies, gt_out)
    ):
        landed = jnp.zeros(head_recv.shape[2:], f32)
        for k, copy in zip(peers, copies):
            copy.wait_recv()
            landed = landed + head_recv[which, k].astype(f32)
        out[:, :main] = value[:high, :main] + landed[:high]
        for low, top, left, right in groups(padded, high):
            out[low:top, main:] = (
                value[low:top, main:] + landed[padded:padded + top - low, left:right])
    for copy in sent:
        if not any(copy is done for done in ts_copies):
            copy.wait_send()


def body(image_features, text_features, image_head, text_head, log_scale, bias):
    rows, depth = image_features.shape
    width = image_head.shape[1]
    n, mp, pair = lax.axis_size("dp"), lax.axis_size("mp"), lax.axis_size("pair")
    shards = mp * pair
    part = rows // shards
    high = depth // n
    padded = -(-high // 16) * 16

    wide = shards * width
    tail = -(-tail_rows(padded, width) // 16) * 16
    main = packing(width)[0]
    scalars = jnp.concatenate([jnp.exp(log_scale), bias])
    vmem = pl.BlockSpec(memory_space=pltpu.VMEM)
    row_loss, gi, gt = pl.pallas_call(
        functools.partial(kernel, n, mp, pair),
        out_shape=(
            jax.ShapeDtypeStruct((1, rows), f32),
            jax.ShapeDtypeStruct((high, width), f32),
            jax.ShapeDtypeStruct((high, width), f32),
        ),
        in_specs=[pl.BlockSpec(memory_space=pltpu.SMEM)] + [vmem] * 4,
        out_specs=(vmem, vmem, vmem),
        scratch_shapes=[
            pltpu.VMEM((rows, width), f32),
            pltpu.VMEM((rows, width), f32),
            pltpu.VMEM((shards, rows, width), bf16),
            pltpu.VMEM((shards, part, width), bf16),
            pltpu.VMEM((shards, part, width), bf16),
            pltpu.VMEM((rows, wide), bf16),
            pltpu.VMEM((2, n, padded, rows), bf16),
            pltpu.VMEM((n, part, wide), bf16),
            pltpu.VMEM((rows, n * part), bf16),
            pltpu.VMEM((shards, rows, width), bf16),
            pltpu.VMEM((shards, rows, width), bf16),
            pltpu.VMEM((n, part, wide), bf16),
            pltpu.VMEM((n, part, wide), bf16),
            pltpu.VMEM((part, wide), f32),
            pltpu.VMEM((shards, part, width), bf16),
            pltpu.VMEM((shards, part, width), bf16),
            pltpu.VMEM((3, 8, rows), f32),
            pltpu.VMEM((3, shards, 8, rows), f32),
            pltpu.VMEM((2, n, padded + tail, main), bf16),
            pltpu.VMEM((2, n, padded + tail, main), bf16),
            pltpu.SemaphoreType.DMA((7, shards)),
            pltpu.SemaphoreType.DMA((7, shards)),
            pltpu.SemaphoreType.DMA((4, n)),
            pltpu.SemaphoreType.DMA((4, n)),
        ],
        compiler_params=pltpu.CompilerParams(
            collective_id=0, has_side_effects=True, vmem_limit_bytes=56 * 1024 * 1024
        ),
    )(
        scalars, image_features, text_features, image_head.T, text_head.T,
    )
    return row_loss.reshape(rows), gi, gt


def solution(mesh):
    in_specs = (
        P(("groups", "dp"), None),
        P(("groups", "dp"), None),
        P(None, ("mp", "pair")),
        P(None, ("mp", "pair")),
        P(),
        P(),
    )
    out_specs = (
        P(("groups", "dp")),
        P(("groups", "dp"), ("mp", "pair")),
        P(("groups", "dp"), ("mp", "pair")),
    )
    return jax.shard_map(body, mesh=mesh, in_specs=in_specs, out_specs=out_specs, check_vma=False)
```

```python
import functools

import jax
import jax.numpy as jnp
from jax import lax
from jax.experimental import pallas as pl
from jax.experimental.pallas import tpu as pltpu
from jax.sharding import PartitionSpec as P

epsilon = 1e-06
f32 = jnp.float32
bf16 = jnp.bfloat16
MESH = pl.DeviceIdType.MESH


def dot_nt(a, b):
    return lax.dot_general(a, b, (((1,), (1,)), ((), ())), preferred_element_type=f32)


def dot_tn(a, b):
    return lax.dot_general(a, b, (((0,), (0,)), ((), ())), preferred_element_type=f32)


def dot_nn(a, b):
    return jnp.dot(a, b, preferred_element_type=f32)


def as_rows(first, second):
    lanes = lax.broadcasted_iota(jnp.int32, (first.shape[0], 128), 1)
    wide = jnp.where(lanes == 0, first, jnp.where(lanes == 1, second, 0.0))
    return wide.T[:8]


def as_columns(block):
    wide = jnp.concatenate([block, jnp.zeros((120, block.shape[1]), f32)], axis=0).T
    return wide[:, 0:1], wide[:, 1:2]


def packing(width):
    main = width // 128 * 128
    rest = width - main

    def groups(padded, high):
        if not rest:
            return []
        step = tail_rows(padded, width)
        starts = range(0, high, step)
        return [
            (low, min(low + step, high), j * rest, (j + 1) * rest) for j, low in enumerate(starts)
        ]

    return main, groups


def tail_rows(padded, width):
    main = width // 128 * 128
    rest = width - main
    return -(-padded // (main // rest * 8)) * 8 if rest else 0


def kernel(
    n, mp, pair,
    log_scale, bias, xi, xt, hi, ht,
    loss_out, gi_out, gt_out,
    unit_i, unit_t, image, text, pieces, wide_image, turned, tall, wall, gi_send, gi_recv, gt_send, gt_recv, own_gt,
    ts_send, ts_recv, stat_send, stat_recv, head_send, head_recv,
    s_send, s_recv, d_send, d_recv,
):
    shards = mp * pair
    rows = xi.shape[0]
    part = rows // shards
    width = hi.shape[0]
    high = gi_out.shape[0]
    my_d = lax.axis_index("dp")
    my_s = lax.axis_index("mp") * pair + lax.axis_index("pair")
    offsets = [0] + [((k + 1) // 2) * (1 if k % 2 else -1) % n for k in range(1, n)]

    def ahead(k):
        return lax.rem(my_d + offsets[k], n)

    def behind(k):
        return lax.rem(my_d + n - offsets[k], n)

    def shard_up(k):
        return lax.rem(my_s + k, shards)

    def shard_down(k):
        return lax.rem(my_s + shards - k, shards)

    def shard_id(s):
        return {"mp": s // pair, "pair": lax.rem(s, pair)}

    def to_shard(src, dst, stage, k, s):
        copy = pltpu.make_async_remote_copy(
            src_ref=src, dst_ref=dst, send_sem=s_send.at[stage, k], recv_sem=s_recv.at[stage, k],
            device_id=shard_id(s), device_id_type=MESH)
        copy.start()
        return copy

    def to_dp(src, dst, stage, k, d):
        copy = pltpu.make_async_remote_copy(
            src_ref=src, dst_ref=dst, send_sem=d_send.at[stage, k], recv_sem=d_recv.at[stage, k],
            device_id={"dp": d}, device_id_type=MESH)
        copy.start()
        return copy

    sent = []
    others = range(1, shards)
    peers = range(1, n)

    barrier = pltpu.get_barrier_semaphore()
    for k in others:
        pl.semaphore_signal(barrier, inc=1, device_id=shard_id(shard_up(k)), device_id_type=MESH)
    for k in peers:
        pl.semaphore_signal(barrier, inc=1, device_id={"dp": ahead(k)}, device_id_type=MESH)

    def stats_start(stage, first, second):
        stat_send[stage] = as_rows(first, second)
        return [
            to_shard(stat_send.at[stage], stat_recv.at[stage, k], stage, k, shard_up(k))
            for k in others
        ]

    def stats_total(stage, copies):
        total = stat_send[stage]
        for k, copy in zip(others, copies):
            copy.wait_recv()
            total = total + stat_recv[stage, k]
        sent.extend(copies)
        return total

    proj_i = dot_nt(xi[...], hi[...])
    proj_t = dot_nt(xt[...], ht[...])
    sq_i = jnp.sum(proj_i * proj_i, axis=1, keepdims=True)
    sq_t = jnp.sum(proj_t * proj_t, axis=1, keepdims=True)
    pl.semaphore_wait(barrier, shards - 1 + n - 1)
    total_i, total_t = as_columns(stats_total(0, stats_start(0, sq_i, sq_t)))
    norm_i = jnp.sqrt(total_i + epsilon)
    norm_t = jnp.sqrt(total_t + epsilon)
    unit_text = proj_t / norm_t
    unit_t[...] = unit_text
    text[...] = unit_text.astype(bf16).reshape(shards, part, width)
    text_copies = [
        to_shard(text.at[shard_up(k)], pieces.at[k], 3, k, shard_up(k)) for k in others
    ]
    tall[0, :, :width] = text[my_s]
    unit_image = proj_i / norm_i
    unit_i[...] = unit_image
    image[0] = unit_image.astype(bf16)
    image_copies = [to_shard(image.at[0], image.at[k], 4, k, shard_up(k)) for k in others]

    for k, copy in zip(others, text_copies):
        copy.wait_recv()
        tall[0, :, k * width:(k + 1) * width] = pieces[k]
    tall_copies = [to_dp(tall.at[0], tall.at[k], 0, k, ahead(k)) for k in peers]
    wide_image[:, :width] = image[0]
    for which, x in enumerate((xi, xt)):
        across = x[...].T
        for e in range(n):
            turned[which, e, :high] = across[e * high:(e + 1) * high]
    for k, copy in zip(others, image_copies):
        copy.wait_recv()
        wide_image[:, k * width:(k + 1) * width] = image[k]
    sent += text_copies + image_copies + tall_copies

    scale = jnp.exp(jnp.full((1, part), log_scale[0], f32))
    offset = bias[0]
    row_ids = lax.broadcasted_iota(jnp.int32, (rows, part), 0)
    col_ids = lax.broadcasted_iota(jnp.int32, (rows, part), 1) + my_s * part
    loss = jnp.zeros((rows, 1), f32)
    inner = jnp.zeros((rows, 1), f32)
    gt_copies = []
    for k in range(n):
        if k:
            tall_copies[k - 1].wait_recv()
        dots = dot_nt(wide_image[...], tall[k])
        logits = scale * dots + offset
        if k == 0:
            flip = jnp.where(row_ids == col_ids, f32(-1.0), f32(1.0))
        else:
            flip = f32(1.0)
        z = flip * logits
        small = jnp.exp(-jnp.abs(z))
        loss = loss + jnp.sum(jnp.maximum(z, 0.0) + jnp.log1p(small), axis=1, keepdims=True)
        sigmoid = jnp.where(z >= 0, f32(1.0), small) / (1.0 + small)
        weights = (flip * sigmoid * (scale / rows)).astype(bf16)
        inner = inner + jnp.sum(weights.astype(f32) * dots, axis=1, keepdims=True)
        wall[:, k * part:(k + 1) * part] = weights
        update = dot_tn(weights, wide_image[...])
        if k == 0:
            own_gt[...] = update
        else:
            gt_send[k] = update.astype(bf16)
            gt_copies.append(to_dp(gt_send.at[k], gt_recv.at[k], 1, k, behind(k)))
    sent += gt_copies
    stat_copies = stats_start(1, inner, loss)

    gi_copies = []
    grad_all = dot_nn(wall[...], tall[...].reshape(n * part, shards * width))
    for j in list(others) + [0]:
        grad = grad_all[:, j * width:(j + 1) * width]
        if j:
            gi_send[j] = grad.astype(bf16)
            gi_copies.append(to_shard(gi_send.at[j], gi_recv.at[j], 5, j, shard_down(j)))
    sent += gi_copies
    for j, copy in zip(others, gi_copies):
        copy.wait_recv()
        grad = grad + gi_recv[j].astype(f32)
    total = stats_total(1, stat_copies)
    loss_out[...] = total[1:2] / (rows * n)
    inner, _ = as_columns(total)
    back_i = ((grad - unit_i[...] * inner) / norm_i).astype(bf16)

    main, groups = packing(width)
    padded = turned.shape[2]

    def head_terms(which, back):
        copies = []
        for k in peers:
            term = dot_nn(turned[which, ahead(k)], back).astype(bf16)
            head_send[which, k, :padded] = term[:, :main]
            for low, top, left, right in groups(padded, padded):
                head_send[which, k, padded:padded + top - low, left:right] = term[low:top, main:]
            copies.append(to_dp(
                head_send.at[which, k], head_recv.at[which, k], 2 + which, k, ahead(k)))
        sent.extend(copies)
        return dot_nn(turned[which, my_d], back), copies

    head_i, head_i_copies = head_terms(0, back_i)

    for copy in gt_copies:
        copy.wait_recv()
    ts_copies = []
    share_all = own_gt[...]
    for k in peers:
        share_all = share_all + gt_recv[k].astype(f32)
    inner_t = jnp.sum(tall[0].astype(f32) * share_all, axis=1, keepdims=True)
    rounded = inner_t.astype(bf16).astype(f32)
    columns = lax.broadcasted_iota(jnp.int32, (part, 2), 1)
    extra = jnp.where(columns == 0, rounded, inner_t - rounded).astype(bf16)
    for j in list(others) + [0]:
        share = share_all[:, j * width:(j + 1) * width]
        if j:
            ts_send[j, :, :width] = share.astype(bf16)
            ts_send[j, :, width:] = extra
            ts_copies.append(to_shard(ts_send.at[j], ts_recv.at[my_s], 6, j, shard_down(j)))
        else:
            ts_recv[my_s, :, :width] = share.astype(bf16)
            ts_recv[my_s, :, width:] = extra
    sent += ts_copies
    for copy in ts_copies:
        copy.wait_send()
    for j in others:
        pltpu.make_async_remote_copy(
            src_ref=ts_send.at[j], dst_ref=ts_recv.at[shard_up(j)], send_sem=s_send.at[6, j],
            recv_sem=s_recv.at[6, j], device_id=shard_id(shard_down(j)), device_id_type=MESH,
        ).wait_recv()
    landed_t = ts_recv[...].reshape(rows, width + 2).astype(f32)
    grad_t = landed_t[:, :width]
    inner_t = landed_t[:, width:width + 1] + landed_t[:, width + 1:]
    back_t = ((grad_t - unit_t[...] * inner_t) / norm_t).astype(bf16)
    head_t, head_t_copies = head_terms(1, back_t)

    for which, value, copies, out in (
        (0, head_i, head_i_copies, gi_out), (1, head_t, head_t_copies, gt_out)
    ):
        landed = jnp.zeros(head_recv.shape[2:], f32)
        for k, copy in zip(peers, copies):
            copy.wait_recv()
            landed = landed + head_recv[which, k].astype(f32)
        out[:, :main] = value[:high, :main] + landed[:high]
        for low, top, left, right in groups(padded, high):
            out[low:top, main:] = (
                value[low:top, main:] + landed[padded:padded + top - low, left:right])
    for copy in sent:
        if not any(copy is done for done in ts_copies):
            copy.wait_send()


def hand_over(loss, gi, gt, loss_out, gi_out, gt_out):
    loss_out[...] = loss[...]
    gi_out[...] = gi[...]
    gt_out[...] = gt[...]


def body(image_features, text_features, image_head, text_head, log_scale, bias):
    rows, depth = image_features.shape
    width = image_head.shape[1]
    n, mp, pair = lax.axis_size("dp"), lax.axis_size("mp"), lax.axis_size("pair")
    shards = mp * pair
    part = rows // shards
    high = depth // n
    padded = -(-high // 16) * 16

    wide = shards * width
    tail = -(-tail_rows(padded, width) // 16) * 16
    main = packing(width)[0]
    smem = pl.BlockSpec(memory_space=pltpu.SMEM)
    vmem = pl.BlockSpec(memory_space=pltpu.VMEM)
    results = pl.pallas_call(
        functools.partial(kernel, n, mp, pair),
        out_shape=(
            jax.ShapeDtypeStruct((1, rows), f32),
            jax.ShapeDtypeStruct((high, width), f32),
            jax.ShapeDtypeStruct((high, width), f32),
        ),
        in_specs=[smem, smem] + [vmem] * 4,
        out_specs=(vmem, vmem, vmem),
        scratch_shapes=[
            pltpu.VMEM((rows, width), f32),
            pltpu.VMEM((rows, width), f32),
            pltpu.VMEM((shards, rows, width), bf16),
            pltpu.VMEM((shards, part, width), bf16),
            pltpu.VMEM((shards, part, width), bf16),
            pltpu.VMEM((rows, wide), bf16),
            pltpu.VMEM((2, n, padded, rows), bf16),
            pltpu.VMEM((n, part, wide), bf16),
            pltpu.VMEM((rows, n * part), bf16),
            pltpu.VMEM((shards, rows, width), bf16),
            pltpu.VMEM((shards, rows, width), bf16),
            pltpu.VMEM((n, part, wide), bf16),
            pltpu.VMEM((n, part, wide), bf16),
            pltpu.VMEM((part, wide), f32),
            pltpu.VMEM((shards, part, width + 2), bf16),
            pltpu.VMEM((shards, part, width + 2), bf16),
            pltpu.VMEM((2, 8, rows), f32),
            pltpu.VMEM((2, shards, 8, rows), f32),
            pltpu.VMEM((2, n, padded + tail, main), bf16),
            pltpu.VMEM((2, n, padded + tail, main), bf16),
            pltpu.SemaphoreType.DMA((7, shards)),
            pltpu.SemaphoreType.DMA((7, shards)),
            pltpu.SemaphoreType.DMA((4, n)),
            pltpu.SemaphoreType.DMA((4, n)),
        ],
        compiler_params=pltpu.CompilerParams(
            collective_id=0, has_side_effects=True, vmem_limit_bytes=56 * 1024 * 1024
        ),
    )(
        log_scale, bias, image_features, text_features, image_head.T, text_head.T,
    )
    row_loss, gi, gt = pl.pallas_call(
        hand_over,
        out_shape=tuple(jax.ShapeDtypeStruct(r.shape, r.dtype) for r in results),
        in_specs=[vmem] * 3,
        out_specs=(vmem, vmem, vmem),
    )(*results)
    return row_loss.reshape(rows), gi, gt


def solution(mesh):
    in_specs = (
        P(("groups", "dp"), None),
        P(("groups", "dp"), None),
        P(None, ("mp", "pair")),
        P(None, ("mp", "pair")),
        P(),
        P(),
    )
    out_specs = (
        P(("groups", "dp")),
        P(("groups", "dp"), ("mp", "pair")),
        P(("groups", "dp"), ("mp", "pair")),
    )
    return jax.shard_map(body, mesh=mesh, in_specs=in_specs, out_specs=out_specs, check_vma=False)
```

```python
import functools

import jax
import jax.numpy as jnp
from jax import lax
from jax.experimental import pallas as pl
from jax.experimental.pallas import tpu as pltpu
from jax.sharding import PartitionSpec as P

epsilon = 1e-06
f32 = jnp.float32
bf16 = jnp.bfloat16
MESH = pl.DeviceIdType.MESH


def dot_nt(a, b):
    return lax.dot_general(a, b, (((1,), (1,)), ((), ())), preferred_element_type=f32)


def dot_tn(a, b):
    return lax.dot_general(a, b, (((0,), (0,)), ((), ())), preferred_element_type=f32)


def dot_nn(a, b):
    return jnp.dot(a, b, preferred_element_type=f32)


def as_rows(first, second):
    lanes = lax.broadcasted_iota(jnp.int32, (first.shape[0], 128), 1)
    wide = jnp.where(lanes == 0, first, jnp.where(lanes == 1, second, 0.0))
    return wide.T[:8]


def as_columns(block):
    wide = jnp.concatenate([block, jnp.zeros((120, block.shape[1]), f32)], axis=0).T
    return wide[:, 0:1], wide[:, 1:2]


def packing(width):
    main = width // 128 * 128
    rest = width - main

    def groups(padded, high):
        if not rest:
            return []
        step = tail_rows(padded, width)
        starts = range(0, high, step)
        return [
            (low, min(low + step, high), j * rest, (j + 1) * rest) for j, low in enumerate(starts)
        ]

    return main, groups


def tail_rows(padded, width):
    main = width // 128 * 128
    rest = width - main
    return -(-padded // (main // rest * 8)) * 8 if rest else 0


def kernel(
    n, mp, pair,
    log_scale, bias, xi, xt, hi, ht,
    loss_out, gi_out, gt_out,
    unit_i, unit_t, image, text, pieces, wide_image, turned, tall, wall, gi_send, gi_recv, gt_send, gt_recv, own_gt,
    ts_send, ts_recv, stat_send, stat_recv, head_send, head_recv,
    s_send, s_recv, d_send, d_recv,
):
    shards = mp * pair
    rows = xi.shape[0]
    part = rows // shards
    width = hi.shape[0]
    high = gi_out.shape[0]
    my_d = lax.axis_index("dp")
    my_s = lax.axis_index("mp") * pair + lax.axis_index("pair")
    offsets = [0] + [((k + 1) // 2) * (1 if k % 2 else -1) % n for k in range(1, n)]

    def ahead(k):
        return lax.rem(my_d + offsets[k], n)

    def behind(k):
        return lax.rem(my_d + n - offsets[k], n)

    def shard_up(k):
        return lax.rem(my_s + k, shards)

    def shard_down(k):
        return lax.rem(my_s + shards - k, shards)

    def shard_id(s):
        return {"mp": s // pair, "pair": lax.rem(s, pair)}

    def to_shard(src, dst, stage, k, s):
        copy = pltpu.make_async_remote_copy(
            src_ref=src, dst_ref=dst, send_sem=s_send.at[stage, k], recv_sem=s_recv.at[stage, k],
            device_id=shard_id(s), device_id_type=MESH)
        copy.start()
        return copy

    def to_dp(src, dst, stage, k, d):
        copy = pltpu.make_async_remote_copy(
            src_ref=src, dst_ref=dst, send_sem=d_send.at[stage, k], recv_sem=d_recv.at[stage, k],
            device_id={"dp": d}, device_id_type=MESH)
        copy.start()
        return copy

    sent = []
    others = range(1, shards)
    peers = range(1, n)

    barrier = pltpu.get_barrier_semaphore()
    for k in others:
        pl.semaphore_signal(barrier, inc=1, device_id=shard_id(shard_up(k)), device_id_type=MESH)
    for k in peers:
        pl.semaphore_signal(barrier, inc=1, device_id={"dp": ahead(k)}, device_id_type=MESH)

    def stats_start(stage, first, second):
        stat_send[stage] = as_rows(first, second)
        return [
            to_shard(stat_send.at[stage], stat_recv.at[stage, k], stage, k, shard_up(k))
            for k in others
        ]

    def stats_total(stage, copies):
        total = stat_send[stage]
        for k, copy in zip(others, copies):
            copy.wait_recv()
            total = total + stat_recv[stage, k]
        sent.extend(copies)
        return total

    proj_i = dot_nt(xi[...], hi[...])
    proj_t = dot_nt(xt[...], ht[...])
    sq_i = jnp.sum(proj_i * proj_i, axis=1, keepdims=True)
    sq_t = jnp.sum(proj_t * proj_t, axis=1, keepdims=True)
    pl.semaphore_wait(barrier, shards - 1 + n - 1)
    total_i, total_t = as_columns(stats_total(0, stats_start(0, sq_i, sq_t)))
    norm_i = jnp.sqrt(total_i + epsilon)
    norm_t = jnp.sqrt(total_t + epsilon)
    unit_text = proj_t / norm_t
    unit_t[...] = unit_text
    text[...] = unit_text.astype(bf16).reshape(shards, part, width)
    text_copies = [
        to_shard(text.at[shard_up(k)], pieces.at[k], 3, k, shard_up(k)) for k in others
    ]
    tall[0, :, :width] = text[my_s]
    unit_image = proj_i / norm_i
    unit_i[...] = unit_image
    image[0] = unit_image.astype(bf16)
    image_copies = [to_shard(image.at[0], image.at[k], 4, k, shard_up(k)) for k in others]

    for k, copy in zip(others, text_copies):
        copy.wait_recv()
        tall[0, :, k * width:(k + 1) * width] = pieces[k]
    tall_copies = [to_dp(tall.at[0], tall.at[k], 0, k, ahead(k)) for k in peers]
    wide_image[:, :width] = image[0]
    for which, x in enumerate((xi, xt)):
        across = x[...].T
        for e in range(n):
            turned[which, e, :high] = across[e * high:(e + 1) * high]
    for k, copy in zip(others, image_copies):
        copy.wait_recv()
        wide_image[:, k * width:(k + 1) * width] = image[k]
    sent += text_copies + image_copies + tall_copies

    scale = jnp.exp(jnp.full((1, part), log_scale[0], f32))
    offset = bias[0]
    row_ids = lax.broadcasted_iota(jnp.int32, (rows, part), 0)
    col_ids = lax.broadcasted_iota(jnp.int32, (rows, part), 1) + my_s * part
    loss = jnp.zeros((rows, 1), f32)
    inner = jnp.zeros((rows, 1), f32)
    gt_copies = []
    for k in range(n):
        if k:
            tall_copies[k - 1].wait_recv()
        dots = dot_nt(wide_image[...], tall[k])
        logits = scale * dots + offset
        if k == 0:
            flip = jnp.where(row_ids == col_ids, f32(-1.0), f32(1.0))
        else:
            flip = f32(1.0)
        z = flip * logits
        small = jnp.exp(-jnp.abs(z))
        loss = loss + jnp.sum(jnp.maximum(z, 0.0) + jnp.log1p(small), axis=1, keepdims=True)
        sigmoid = jnp.where(z >= 0, f32(1.0), small) / (1.0 + small)
        weights = (flip * sigmoid * (scale / rows)).astype(bf16)
        inner = inner + jnp.sum(weights.astype(f32) * dots, axis=1, keepdims=True)
        wall[:, k * part:(k + 1) * part] = weights
        update = dot_tn(weights, wide_image[...])
        if k == 0:
            own_gt[...] = update
        else:
            gt_send[k] = update.astype(bf16)
            gt_copies.append(to_dp(gt_send.at[k], gt_recv.at[k], 1, k, behind(k)))
    sent += gt_copies
    stat_copies = stats_start(1, inner, loss)

    gi_copies = []
    grad_all = dot_nn(wall[...], tall[...].reshape(n * part, shards * width))
    for j in list(others) + [0]:
        grad = grad_all[:, j * width:(j + 1) * width]
        if j:
            gi_send[j] = grad.astype(bf16)
            gi_copies.append(to_shard(gi_send.at[j], gi_recv.at[j], 5, j, shard_down(j)))
    sent += gi_copies
    for j, copy in zip(others, gi_copies):
        copy.wait_recv()
        grad = grad + gi_recv[j].astype(f32)
    total = stats_total(1, stat_copies)
    loss_out[...] = total[1:2] / (rows * n)
    inner, _ = as_columns(total)
    back_i = ((grad - unit_i[...] * inner) / norm_i).astype(bf16)

    main, groups = packing(width)
    padded = turned.shape[2]

    def head_terms(which, back):
        copies = []
        for k in reversed(peers):
            term = dot_nn(turned[which, ahead(k)], back).astype(bf16)
            head_send[which, k, :padded] = term[:, :main]
            for low, top, left, right in groups(padded, padded):
                head_send[which, k, padded:padded + top - low, left:right] = term[low:top, main:]
            copies.append(to_dp(
                head_send.at[which, k], head_recv.at[which, k], 2 + which, k, ahead(k)))
        sent.extend(copies)
        copies.reverse()
        return dot_nn(turned[which, my_d], back), copies

    head_i, head_i_copies = head_terms(0, back_i)

    for copy in gt_copies:
        copy.wait_recv()
    ts_copies = []
    share_all = own_gt[...]
    for k in peers:
        share_all = share_all + gt_recv[k].astype(f32)
    inner_t = jnp.sum(tall[0].astype(f32) * share_all, axis=1, keepdims=True)
    rounded = inner_t.astype(bf16).astype(f32)
    columns = lax.broadcasted_iota(jnp.int32, (part, 2), 1)
    extra = jnp.where(columns == 0, rounded, inner_t - rounded).astype(bf16)
    for j in list(others) + [0]:
        share = share_all[:, j * width:(j + 1) * width]
        if j:
            ts_send[j, :, :width] = share.astype(bf16)
            ts_send[j, :, width:] = extra
            ts_copies.append(to_shard(ts_send.at[j], ts_recv.at[my_s], 6, j, shard_down(j)))
        else:
            ts_recv[my_s, :, :width] = share.astype(bf16)
            ts_recv[my_s, :, width:] = extra
    sent += ts_copies
    for copy in ts_copies:
        copy.wait_send()
    for j in others:
        pltpu.make_async_remote_copy(
            src_ref=ts_send.at[j], dst_ref=ts_recv.at[shard_up(j)], send_sem=s_send.at[6, j],
            recv_sem=s_recv.at[6, j], device_id=shard_id(shard_down(j)), device_id_type=MESH,
        ).wait_recv()
    landed_t = ts_recv[...].reshape(rows, width + 2).astype(f32)
    grad_t = landed_t[:, :width]
    inner_t = landed_t[:, width:width + 1] + landed_t[:, width + 1:]
    back_t = ((grad_t - unit_t[...] * inner_t) / norm_t).astype(bf16)
    head_t, head_t_copies = head_terms(1, back_t)

    for which, value, copies, out in (
        (0, head_i, head_i_copies, gi_out), (1, head_t, head_t_copies, gt_out)
    ):
        landed = jnp.zeros(head_recv.shape[2:], f32)
        for k, copy in zip(peers, copies):
            copy.wait_recv()
            landed = landed + head_recv[which, k].astype(f32)
        out[:, :main] = value[:high, :main] + landed[:high]
        for low, top, left, right in groups(padded, high):
            out[low:top, main:] = (
                value[low:top, main:] + landed[padded:padded + top - low, left:right])
    for copy in sent:
        if not any(copy is done for done in ts_copies):
            copy.wait_send()


def hand_over(loss, gi, gt, loss_out, gi_out, gt_out):
    loss_out[...] = loss[...]
    gi_out[...] = gi[...]
    gt_out[...] = gt[...]


def body(image_features, text_features, image_head, text_head, log_scale, bias):
    rows, depth = image_features.shape
    width = image_head.shape[1]
    n, mp, pair = lax.axis_size("dp"), lax.axis_size("mp"), lax.axis_size("pair")
    shards = mp * pair
    part = rows // shards
    high = depth // n
    padded = -(-high // 16) * 16

    wide = shards * width
    tail = -(-tail_rows(padded, width) // 16) * 16
    main = packing(width)[0]
    smem = pl.BlockSpec(memory_space=pltpu.SMEM)
    vmem = pl.BlockSpec(memory_space=pltpu.VMEM)
    results = pl.pallas_call(
        functools.partial(kernel, n, mp, pair),
        out_shape=(
            jax.ShapeDtypeStruct((1, rows), f32),
            jax.ShapeDtypeStruct((high, width), f32),
            jax.ShapeDtypeStruct((high, width), f32),
        ),
        in_specs=[smem, smem] + [vmem] * 4,
        out_specs=(vmem, vmem, vmem),
        scratch_shapes=[
            pltpu.VMEM((rows, width), f32),
            pltpu.VMEM((rows, width), f32),
            pltpu.VMEM((shards, rows, width), bf16),
            pltpu.VMEM((shards, part, width), bf16),
            pltpu.VMEM((shards, part, width), bf16),
            pltpu.VMEM((rows, wide), bf16),
            pltpu.VMEM((2, n, padded, rows), bf16),
            pltpu.VMEM((n, part, wide), bf16),
            pltpu.VMEM((rows, n * part), bf16),
            pltpu.VMEM((shards, rows, width), bf16),
            pltpu.VMEM((shards, rows, width), bf16),
            pltpu.VMEM((n, part, wide), bf16),
            pltpu.VMEM((n, part, wide), bf16),
            pltpu.VMEM((part, wide), f32),
            pltpu.VMEM((shards, part, width + 2), bf16),
            pltpu.VMEM((shards, part, width + 2), bf16),
            pltpu.VMEM((2, 8, rows), f32),
            pltpu.VMEM((2, shards, 8, rows), f32),
            pltpu.VMEM((2, n, padded + tail, main), bf16),
            pltpu.VMEM((2, n, padded + tail, main), bf16),
            pltpu.SemaphoreType.DMA((7, shards)),
            pltpu.SemaphoreType.DMA((7, shards)),
            pltpu.SemaphoreType.DMA((4, n)),
            pltpu.SemaphoreType.DMA((4, n)),
        ],
        compiler_params=pltpu.CompilerParams(
            collective_id=0, has_side_effects=True, vmem_limit_bytes=56 * 1024 * 1024
        ),
    )(
        log_scale, bias, image_features, text_features, image_head.T, text_head.T,
    )
    row_loss, gi, gt = pl.pallas_call(
        hand_over,
        out_shape=tuple(jax.ShapeDtypeStruct(r.shape, r.dtype) for r in results),
        in_specs=[vmem] * 3,
        out_specs=(vmem, vmem, vmem),
    )(*results)
    return row_loss.reshape(rows), gi, gt


def solution(mesh):
    in_specs = (
        P(("groups", "dp"), None),
        P(("groups", "dp"), None),
        P(None, ("mp", "pair")),
        P(None, ("mp", "pair")),
        P(),
        P(),
    )
    out_specs = (
        P(("groups", "dp")),
        P(("groups", "dp"), ("mp", "pair")),
        P(("groups", "dp"), ("mp", "pair")),
    )
    return jax.shard_map(body, mesh=mesh, in_specs=in_specs, out_specs=out_specs, check_vma=False)
```

```python
import functools

import jax
import jax.numpy as jnp
from jax import lax
from jax.experimental import pallas as pl
from jax.experimental.pallas import tpu as pltpu
from jax.sharding import PartitionSpec as P

epsilon = 1e-06
f32 = jnp.float32
bf16 = jnp.bfloat16
MESH = pl.DeviceIdType.MESH


def dot_nt(a, b):
    return lax.dot_general(a, b, (((1,), (1,)), ((), ())), preferred_element_type=f32)


def dot_tn(a, b):
    return lax.dot_general(a, b, (((0,), (0,)), ((), ())), preferred_element_type=f32)


def dot_nn(a, b):
    return jnp.dot(a, b, preferred_element_type=f32)


def as_rows(first, second):
    lanes = lax.broadcasted_iota(jnp.int32, (first.shape[0], 128), 1)
    wide = jnp.where(lanes == 0, first, jnp.where(lanes == 1, second, 0.0))
    return wide.T[:8]


def as_columns(block):
    wide = jnp.concatenate([block, jnp.zeros((120, block.shape[1]), f32)], axis=0).T
    return wide[:, 0:1], wide[:, 1:2]


def packing(width):
    main = width // 128 * 128
    rest = width - main

    def groups(padded, high):
        if not rest:
            return []
        step = tail_rows(padded, width)
        starts = range(0, high, step)
        return [
            (low, min(low + step, high), j * rest, (j + 1) * rest) for j, low in enumerate(starts)
        ]

    return main, groups


def tail_rows(padded, width):
    main = width // 128 * 128
    rest = width - main
    return -(-padded // (main // rest * 8)) * 8 if rest else 0


def kernel(
    n, mp, pair,
    log_scale, bias, xi, xt, hi, ht,
    loss_out, gi_out, gt_out,
    unit_i, unit_t, image, text, pieces, wide_image, turned, tall, wall, gi_send, gi_recv, gt_send, gt_recv, own_gt,
    ts_send, ts_recv, stat_send, stat_recv, head_send, head_recv,
    s_send, s_recv, d_send, d_recv,
):
    shards = mp * pair
    rows = xi.shape[0]
    part = rows // shards
    width = hi.shape[0]
    high = gi_out.shape[0]
    my_d = lax.axis_index("dp")
    my_s = lax.axis_index("mp") * pair + lax.axis_index("pair")
    offsets = [0] + [((k + 1) // 2) * (1 if k % 2 else -1) % n for k in range(1, n)]

    def ahead(k):
        return lax.rem(my_d + offsets[k], n)

    def behind(k):
        return lax.rem(my_d + n - offsets[k], n)

    def shard_up(k):
        return lax.rem(my_s + k, shards)

    def shard_down(k):
        return lax.rem(my_s + shards - k, shards)

    def shard_id(s):
        return {"mp": s // pair, "pair": lax.rem(s, pair)}

    def to_shard(src, dst, stage, k, s):
        copy = pltpu.make_async_remote_copy(
            src_ref=src, dst_ref=dst, send_sem=s_send.at[stage, k], recv_sem=s_recv.at[stage, k],
            device_id=shard_id(s), device_id_type=MESH)
        copy.start()
        return copy

    def to_dp(src, dst, stage, k, d):
        copy = pltpu.make_async_remote_copy(
            src_ref=src, dst_ref=dst, send_sem=d_send.at[stage, k], recv_sem=d_recv.at[stage, k],
            device_id={"dp": d}, device_id_type=MESH)
        copy.start()
        return copy

    sent = []
    others = range(1, shards)
    peers = range(1, n)

    barrier = pltpu.get_barrier_semaphore()
    for k in others:
        pl.semaphore_signal(barrier, inc=1, device_id=shard_id(shard_up(k)), device_id_type=MESH)
    for k in peers:
        pl.semaphore_signal(barrier, inc=1, device_id={"dp": ahead(k)}, device_id_type=MESH)

    def stats_start(stage, first, second):
        stat_send[stage] = as_rows(first, second)
        return [
            to_shard(stat_send.at[stage], stat_recv.at[stage, k], stage, k, shard_up(k))
            for k in others
        ]

    def stats_total(stage, copies):
        total = stat_send[stage]
        for k, copy in zip(others, copies):
            copy.wait_recv()
            total = total + stat_recv[stage, k]
        sent.extend(copies)
        return total

    proj_i = dot_nt(xi[...], hi[...])
    proj_t = dot_nt(xt[...], ht[...])
    sq_i = jnp.sum(proj_i * proj_i, axis=1, keepdims=True)
    sq_t = jnp.sum(proj_t * proj_t, axis=1, keepdims=True)
    pl.semaphore_wait(barrier, shards - 1 + n - 1)
    total_i, total_t = as_columns(stats_total(0, stats_start(0, sq_i, sq_t)))
    norm_i = jnp.sqrt(total_i + epsilon)
    norm_t = jnp.sqrt(total_t + epsilon)
    unit_text = proj_t / norm_t
    unit_t[...] = unit_text
    text[...] = unit_text.astype(bf16).reshape(shards, part, width)
    text_copies = [
        to_shard(text.at[shard_up(k)], pieces.at[k], 3, k, shard_up(k)) for k in others
    ]
    tall[0, :, :width] = text[my_s]
    unit_image = proj_i / norm_i
    unit_i[...] = unit_image
    image[0] = unit_image.astype(bf16)
    image_copies = [to_shard(image.at[0], image.at[k], 4, k, shard_up(k)) for k in others]

    for k, copy in zip(others, text_copies):
        copy.wait_recv()
        tall[0, :, k * width:(k + 1) * width] = pieces[k]
    tall_copies = [to_dp(tall.at[0], tall.at[k], 0, k, ahead(k)) for k in reversed(peers)]
    tall_copies.reverse()
    wide_image[:, :width] = image[0]
    for which, x in enumerate((xi, xt)):
        across = x[...].T
        for e in range(n):
            turned[which, e, :high] = across[e * high:(e + 1) * high]
    for k, copy in zip(others, image_copies):
        copy.wait_recv()
        wide_image[:, k * width:(k + 1) * width] = image[k]
    sent += text_copies + image_copies + tall_copies

    scale = jnp.exp(jnp.full((1, part), log_scale[0], f32))
    offset = bias[0]
    row_ids = lax.broadcasted_iota(jnp.int32, (rows, part), 0)
    col_ids = lax.broadcasted_iota(jnp.int32, (rows, part), 1) + my_s * part
    loss = jnp.zeros((rows, 1), f32)
    inner = jnp.zeros((rows, 1), f32)
    gt_copies = []
    for k in range(n):
        if k:
            tall_copies[k - 1].wait_recv()
        dots = dot_nt(wide_image[...], tall[k])
        logits = scale * dots + offset
        if k == 0:
            flip = jnp.where(row_ids == col_ids, f32(-1.0), f32(1.0))
        else:
            flip = f32(1.0)
        z = flip * logits
        small = jnp.exp(-jnp.abs(z))
        loss = loss + jnp.sum(jnp.maximum(z, 0.0) + jnp.log1p(small), axis=1, keepdims=True)
        sigmoid = jnp.where(z >= 0, f32(1.0), small) / (1.0 + small)
        weights = (flip * sigmoid * (scale / rows)).astype(bf16)
        inner = inner + jnp.sum(weights.astype(f32) * dots, axis=1, keepdims=True)
        wall[:, k * part:(k + 1) * part] = weights
        update = dot_tn(weights, wide_image[...])
        if k == 0:
            own_gt[...] = update
        else:
            gt_send[k] = update.astype(bf16)
            gt_copies.append(to_dp(gt_send.at[k], gt_recv.at[k], 1, k, behind(k)))
    sent += gt_copies
    stat_copies = stats_start(1, inner, loss)

    gi_copies = []
    grad_all = dot_nn(wall[...], tall[...].reshape(n * part, shards * width))
    for j in list(others) + [0]:
        grad = grad_all[:, j * width:(j + 1) * width]
        if j:
            gi_send[j] = grad.astype(bf16)
            gi_copies.append(to_shard(gi_send.at[j], gi_recv.at[j], 5, j, shard_down(j)))
    sent += gi_copies
    for j, copy in zip(others, gi_copies):
        copy.wait_recv()
        grad = grad + gi_recv[j].astype(f32)
    total = stats_total(1, stat_copies)
    loss_out[...] = total[1:2] / (rows * n)
    inner, _ = as_columns(total)
    back_i = ((grad - unit_i[...] * inner) / norm_i).astype(bf16)

    main, groups = packing(width)
    padded = turned.shape[2]

    def head_terms(which, back):
        copies = []
        for k in reversed(peers):
            term = dot_nn(turned[which, ahead(k)], back).astype(bf16)
            head_send[which, k, :padded] = term[:, :main]
            for low, top, left, right in groups(padded, padded):
                head_send[which, k, padded:padded + top - low, left:right] = term[low:top, main:]
            copies.append(to_dp(
                head_send.at[which, k], head_recv.at[which, k], 2 + which, k, ahead(k)))
        sent.extend(copies)
        copies.reverse()
        return dot_nn(turned[which, my_d], back), copies

    head_i, head_i_copies = head_terms(0, back_i)

    for copy in gt_copies:
        copy.wait_recv()
    ts_copies = []
    share_all = own_gt[...]
    for k in peers:
        share_all = share_all + gt_recv[k].astype(f32)
    inner_t = jnp.sum(tall[0].astype(f32) * share_all, axis=1, keepdims=True)
    rounded = inner_t.astype(bf16).astype(f32)
    columns = lax.broadcasted_iota(jnp.int32, (part, 2), 1)
    extra = jnp.where(columns == 0, rounded, inner_t - rounded).astype(bf16)
    for j in list(others) + [0]:
        share = share_all[:, j * width:(j + 1) * width]
        if j:
            ts_send[j, :, :width] = share.astype(bf16)
            ts_send[j, :, width:] = extra
            ts_copies.append(to_shard(ts_send.at[j], ts_recv.at[my_s], 6, j, shard_down(j)))
        else:
            ts_recv[my_s, :, :width] = share.astype(bf16)
            ts_recv[my_s, :, width:] = extra
    sent += ts_copies
    for copy in ts_copies:
        copy.wait_send()
    for j in others:
        pltpu.make_async_remote_copy(
            src_ref=ts_send.at[j], dst_ref=ts_recv.at[shard_up(j)], send_sem=s_send.at[6, j],
            recv_sem=s_recv.at[6, j], device_id=shard_id(shard_down(j)), device_id_type=MESH,
        ).wait_recv()
    landed_t = ts_recv[...].reshape(rows, width + 2).astype(f32)
    grad_t = landed_t[:, :width]
    inner_t = landed_t[:, width:width + 1] + landed_t[:, width + 1:]
    back_t = ((grad_t - unit_t[...] * inner_t) / norm_t).astype(bf16)
    head_t, head_t_copies = head_terms(1, back_t)

    for which, value, copies, out in (
        (0, head_i, head_i_copies, gi_out), (1, head_t, head_t_copies, gt_out)
    ):
        landed = jnp.zeros(head_recv.shape[2:], f32)
        for k, copy in zip(peers, copies):
            copy.wait_recv()
            landed = landed + head_recv[which, k].astype(f32)
        out[:, :main] = value[:high, :main] + landed[:high]
        for low, top, left, right in groups(padded, high):
            out[low:top, main:] = (
                value[low:top, main:] + landed[padded:padded + top - low, left:right])
    for copy in sent:
        if not any(copy is done for done in ts_copies):
            copy.wait_send()


def hand_over(loss, gi, gt, loss_out, gi_out, gt_out):
    loss_out[...] = loss[...]
    gi_out[...] = gi[...]
    gt_out[...] = gt[...]


def body(image_features, text_features, image_head, text_head, log_scale, bias):
    rows, depth = image_features.shape
    width = image_head.shape[1]
    n, mp, pair = lax.axis_size("dp"), lax.axis_size("mp"), lax.axis_size("pair")
    shards = mp * pair
    part = rows // shards
    high = depth // n
    padded = -(-high // 16) * 16

    wide = shards * width
    tail = -(-tail_rows(padded, width) // 16) * 16
    main = packing(width)[0]
    smem = pl.BlockSpec(memory_space=pltpu.SMEM)
    vmem = pl.BlockSpec(memory_space=pltpu.VMEM)
    results = pl.pallas_call(
        functools.partial(kernel, n, mp, pair),
        out_shape=(
            jax.ShapeDtypeStruct((1, rows), f32),
            jax.ShapeDtypeStruct((high, width), f32),
            jax.ShapeDtypeStruct((high, width), f32),
        ),
        in_specs=[smem, smem] + [vmem] * 4,
        out_specs=(vmem, vmem, vmem),
        scratch_shapes=[
            pltpu.VMEM((rows, width), f32),
            pltpu.VMEM((rows, width), f32),
            pltpu.VMEM((shards, rows, width), bf16),
            pltpu.VMEM((shards, part, width), bf16),
            pltpu.VMEM((shards, part, width), bf16),
            pltpu.VMEM((rows, wide), bf16),
            pltpu.VMEM((2, n, padded, rows), bf16),
            pltpu.VMEM((n, part, wide), bf16),
            pltpu.VMEM((rows, n * part), bf16),
            pltpu.VMEM((shards, rows, width), bf16),
            pltpu.VMEM((shards, rows, width), bf16),
            pltpu.VMEM((n, part, wide), bf16),
            pltpu.VMEM((n, part, wide), bf16),
            pltpu.VMEM((part, wide), f32),
            pltpu.VMEM((shards, part, width + 2), bf16),
            pltpu.VMEM((shards, part, width + 2), bf16),
            pltpu.VMEM((2, 8, rows), f32),
            pltpu.VMEM((2, shards, 8, rows), f32),
            pltpu.VMEM((2, n, padded + tail, main), bf16),
            pltpu.VMEM((2, n, padded + tail, main), bf16),
            pltpu.SemaphoreType.DMA((7, shards)),
            pltpu.SemaphoreType.DMA((7, shards)),
            pltpu.SemaphoreType.DMA((4, n)),
            pltpu.SemaphoreType.DMA((4, n)),
        ],
        compiler_params=pltpu.CompilerParams(
            collective_id=0, has_side_effects=True, vmem_limit_bytes=56 * 1024 * 1024
        ),
    )(
        log_scale, bias, image_features, text_features, image_head.T, text_head.T,
    )
    row_loss, gi, gt = pl.pallas_call(
        hand_over,
        out_shape=tuple(jax.ShapeDtypeStruct(r.shape, r.dtype) for r in results),
        in_specs=[vmem] * 3,
        out_specs=(vmem, vmem, vmem),
    )(*results)
    return row_loss.reshape(rows), gi, gt


def solution(mesh):
    in_specs = (
        P(("groups", "dp"), None),
        P(("groups", "dp"), None),
        P(None, ("mp", "pair")),
        P(None, ("mp", "pair")),
        P(),
        P(),
    )
    out_specs = (
        P(("groups", "dp")),
        P(("groups", "dp"), ("mp", "pair")),
        P(("groups", "dp"), ("mp", "pair")),
    )
    return jax.shard_map(body, mesh=mesh, in_specs=in_specs, out_specs=out_specs, check_vma=False)
```
